32 devices in a mesh: gx: 8 (over z, y), gz: 4 (over x, core).
Axes of the slice: x: 2, y: 2, z: 4, core: 2. Of those that a mesh axis runs over, the one named last changes fastest.
Arguments:
- whitened: float32 [2, 64, 1024, 512], P(None, 'gz', 'gx'), may hold values from -6 to 6
- observed: float32 [2, 1024, 512], P(None, 'gx'), may hold values from -12 to 12
- lower_x: bfloat16 [1024, 1024], P('gx'), as said below
- lower_y: bfloat16 [512, 512], P('gx'), as said below
- lower_z: bfloat16 [64, 64], replicated, as said below
- coupling_kernel: float32 [2, 3, 3, 3], replicated, may hold values from -1.25 to 1.25
Outputs:
- gradient: float32 [2, 64, 1024, 512], P(None, 'gz', 'gx')
- misfit: float32 [2, 1024, 512], P(None, 'gx')
The draws below stay inside these ranges and needn't reach their ends.
Inputs may be any that keep to these rules, and one draw needn't show every extreme that they name: `lower_x`: lower triangular: zero above the diagonal, diagonal entries between 0.5 and 1.5. `lower_y`: lower triangular: zero above the diagonal, diagonal entries between 0.5 and 1.5. `lower_z`: lower triangular: zero above the diagonal, diagonal entries between 0.5 and 1.5.
All inputs are finite; a program needn't handle non-finite values.
Results may differ from the reference program's by a relative error of at most 0.013.
The reference program's roundings to bfloat16 on the way count: a program that leaves them out, or rounds other values in their place, can miss the bound.
Values may be sent and summed in bfloat16 or wider, within the bound.
A program may use at most 128 MiB of HBM per device.

```python
import math
import jax
import jax.numpy as jnp
from jax import lax

NX = 1024
NY = 512
NZ = 64


def lower_draw(key, order):
    first_key, second_key = jax.random.split(key)
    spread = jnp.clip(jax.random.normal(first_key, (order, order), jnp.float32), -4.0, 4.0)
    diagonal = jax.random.uniform(second_key, (order,), jnp.float32, 0.6, 1.4)
    rows = lax.broadcasted_iota(jnp.int32, (order, order), 0)
    columns = lax.broadcasted_iota(jnp.int32, (order, order), 1)
    below = jnp.where(rows > columns, spread / math.sqrt(order), 0.0)
    on_diag = jnp.where(rows == columns, diagonal[:, None], 0.0)
    return (below + on_diag).astype(jnp.bfloat16)


def draw_lower_x(key, part):
    return lower_draw(jax.random.fold_in(key, 11), NX)


def draw_lower_y(key, part):
    return lower_draw(jax.random.fold_in(key, 23), NY)


def draw_lower_z(key, part):
    return lower_draw(jax.random.fold_in(key, 37), NZ)


def block_levels(stream_key, dims, cuts, least, high):
    factor_of = 1.0
    for position, parts in cuts:
        steps = jax.random.uniform(jax.random.fold_in(jax.random.fold_in(stream_key, 6), position), (parts,), jnp.float32, least / len(cuts), high / len(cuts))
        factor_of = factor_of * jnp.repeat(jnp.exp(steps), dims[position] // parts).reshape((-1,) + (1,) * (len(dims) - 1 - position))
    return factor_of


def normal_values(key, shape, scale, limit, shards=(), kind=jnp.bfloat16):
    drawn = scale * jax.random.normal(key, shape, jnp.float32)
    if shards:
        drawn = drawn * block_levels(key, shape, shards, -0.22, 0.18)
    return jnp.clip(drawn, -limit, limit).astype(kind)


def setup_inputs(seed: int = 0) -> dict:
    seeds = jax.random.split(jax.random.key(seed), 7)
    whitened = normal_values(seeds[0], (2, NZ, NX, NY), 1.0, 6.0, ((1, 4), (2, 8)), jnp.float32)
    observed = normal_values(seeds[1], (2, NX, NY), 2.0, 12.0, ((1, 8),), jnp.float32)
    lower_x = draw_lower_x(jax.random.fold_in(seeds[6], 71), 0)
    lower_y = draw_lower_y(jax.random.fold_in(seeds[6], 71), 0)
    lower_z = draw_lower_z(jax.random.fold_in(seeds[6], 71), 0)
    coupling_kernel = normal_values(seeds[5], (2, 3, 3, 3), 27 ** -0.5, 1.25, (), jnp.float32)
    return dict(whitened=whitened, observed=observed, lower_x=lower_x, lower_y=lower_y, lower_z=lower_z, coupling_kernel=coupling_kernel)


def prior_forward(field, fx, fy, fz):
    first = jnp.einsum('zxk,yk->zxy', field.astype(jnp.float32), fy).astype(jnp.bfloat16)
    second = jnp.einsum('zk,kxy->zxy', fz, first.astype(jnp.float32)).astype(jnp.bfloat16)
    return jnp.einsum('xk,zky->zxy', fx, second.astype(jnp.float32)).astype(jnp.bfloat16)

def prior_backward(field, fx, fy, fz):
    third = jnp.einsum('kx,zky->zxy', fx, field.astype(jnp.float32)).astype(jnp.bfloat16)
    fourth = jnp.einsum('kz,kxy->zxy', fz, third.astype(jnp.float32)).astype(jnp.bfloat16)
    return jnp.einsum('zxk,ky->zxy', fourth.astype(jnp.float32), fy)

def stencil(field, kernel):
    padded = jnp.pad(field.astype(jnp.float32), 1)
    total = jnp.zeros(field.shape, jnp.float32)
    for offset_z in range(3):
        for offset_x in range(3):
            for offset_y in range(3):
                total = total + kernel[offset_z, offset_x, offset_y] * padded[offset_z:offset_z + NZ, offset_x:offset_x + NX, offset_y:offset_y + NY]
    return total

def stencil_adjoint(field, kernel):
    padded = jnp.pad(field.astype(jnp.float32), 1)
    total = jnp.zeros(field.shape, jnp.float32)
    for offset_z in range(3):
        for offset_x in range(3):
            for offset_y in range(3):
                total = total + kernel[offset_z, offset_x, offset_y] * padded[2 - offset_z:2 - offset_z + NZ, 2 - offset_x:2 - offset_x + NX, 2 - offset_y:2 - offset_y + NY]
    return total

def reference(whitened, observed, lower_x, lower_y, lower_z, coupling_kernel):
    fx = lower_x.astype(jnp.float32)
    fy = lower_y.astype(jnp.float32)
    fz = lower_z.astype(jnp.float32)
    start = whitened.astype(jnp.bfloat16)
    density = prior_forward(start[0], fx, fy, fz)
    magnetic = prior_forward(start[1], fx, fy, fz)
    pre_scale = stencil(density, coupling_kernel[0])
    pre_shift = stencil(density, coupling_kernel[1])
    scale = jnp.tanh(pre_scale)
    growth = jnp.exp(scale)
    magnetic_f = magnetic.astype(jnp.float32)
    coupled = magnetic_f * growth + pre_shift
    depth = jnp.arange(NZ, dtype=jnp.float32)
    factor = 4.0 / jnp.sqrt(jnp.float32(NZ))
    weight_g = factor / (1.0 + depth / NZ) ** 2
    weight_m = factor / (1.0 + depth / NZ) ** 3
    pred_g = jnp.einsum('z,zxy->xy', weight_g, density.astype(jnp.float32))
    pred_m = jnp.einsum('z,zxy->xy', weight_m, coupled)
    misfit = jnp.stack([pred_g, pred_m]) - observed
    back_g = weight_g[:, None, None] * misfit[0][None]
    back_m = weight_m[:, None, None] * misfit[1][None]
    back_scale = (back_m * magnetic_f * growth * (1.0 - scale * scale)).astype(jnp.bfloat16)
    back_shift = back_m.astype(jnp.bfloat16)
    adj_g = (back_g + stencil_adjoint(back_scale, coupling_kernel[0]) + stencil_adjoint(back_shift, coupling_kernel[1])).astype(jnp.bfloat16)
    adj_m = (back_m * growth).astype(jnp.bfloat16)
    grad_g = prior_backward(adj_g, fx, fy, fz)
    grad_m = prior_backward(adj_m, fx, fy, fz)
    gradient = whitened + jnp.stack([grad_g, grad_m])
    return (gradient, misfit)
```

```python
import math

import jax
import jax.numpy as jnp
from jax import lax
from jax.experimental import pallas as pl
from jax.experimental.pallas import tpu as pltpu
from jax.sharding import PartitionSpec as P

NZ = 64


def padded_2(x, sides, width):
    for axis, dim in sides:
        peers, length = (lax.axis_size(axis), x.shape[dim])
        up = [(i, (i + 1) % peers) for i in range(peers - 1)]
        down = [(j, i) for i, j in up]
        last = lax.slice_in_dim(x, length - width, length, axis=dim)
        first = lax.slice_in_dim(x, 0, width, axis=dim)
        before = lax.ppermute(last, axis, up)
        after = lax.ppermute(first, axis, down)
        x = jnp.concatenate([before, x, after], axis=dim)
    return x


def depth_lines(values, local_step):
    turned = lax.all_to_all(values, "gz", split_axis=2, concat_axis=1, tiled=True)
    return lax.all_to_all(local_step(turned), "gz", split_axis=1, concat_axis=2, tiled=True)


def across_lines(values, local_step):
    fields, depth, rows, cols = values.shape
    if (fields * depth) % lax.axis_size("gx"):
        turned = lax.all_to_all(values, "gx", split_axis=3, concat_axis=2, tiled=True)
        return lax.all_to_all(local_step(turned), "gx", split_axis=2, concat_axis=3, tiled=True)
    planes = values.reshape(1, fields * depth, rows, cols)
    turned = lax.all_to_all(planes, "gx", split_axis=1, concat_axis=2, tiled=True)
    back = lax.all_to_all(local_step(turned), "gx", split_axis=2, concat_axis=1, tiled=True)
    return back.reshape(values.shape)


CHUNK = 16
EDGE = 8


def edge_padded(rim):
    sides = ((EDGE - 1, EDGE - 1), (0, 0))
    return jnp.pad(rim, ((0, 0),) * (rim.ndim - 2) + sides).astype(jnp.float32)


def beside(low, high, middle):
    cols = middle.shape[1]
    lane = lax.broadcasted_iota(jnp.int32, middle.shape, 1)
    before = jnp.where(lane == 0, 0.0, pltpu.roll(low, 1, 1))
    after = jnp.where(lane == cols - 1, 0.0, pltpu.roll(high, cols - 1, 1))
    return middle + before + after


def forward_kernel(taps, weights, p0, p1, p2, magnetic, growth_out, slope_out, sums):
    z = pl.program_id(0)
    planes = (p0, p1, p2)
    weight_g, weight_m = weights[0, z], weights[1, z]

    @pl.when(z == 0)
    def _():
        sums[...] = jnp.zeros_like(sums)

    def part(row, mag):
        acc = [None] * 6
        for a in range(3):
            for b in range(3):
                at = row + EDGE - 1 + b
                v = planes[a][0, at : at + 8, :]
                for c in range(2):
                    for e in range(3):
                        term = taps[27 * c + 9 * a + 3 * b + e] * v
                        i = 3 * c + e
                        acc[i] = term if acc[i] is None else acc[i] + term
        scale = jnp.tanh(beside(acc[0], acc[2], acc[1]))
        shift = beside(acc[3], acc[5], acc[4])
        growth = jnp.exp(scale)
        out = slice(row, row + 8)
        growth_out[0, out, :] = growth
        slope_out[0, out, :] = mag * growth * (1.0 - scale * scale)
        density = p1[0, row + EDGE : row + EDGE + 8, :]
        sums[0, out, :] += weight_g * density
        sums[1, out, :] += weight_m * (mag * growth + shift)

    for row in range(0, magnetic.shape[1], CHUNK):
        mag = magnetic[0, row : row + CHUNK, :].astype(jnp.float32)
        part(row, mag[:8])
        part(row + 8, mag[8:])


def backward_kernel(taps, weights, p0, p1, p2, growth, misfit, out_ref):
    z = pl.program_id(0)
    planes = (p2, p1, p0)
    weight_g, weight_m = weights[0, z], weights[1, z]

    def part(row):
        acc = [None] * 3
        for c in range(2):
            for a in range(3):
                for b in range(3):
                    at = row + EDGE + 1 - b
                    v = planes[a][c, 0, at : at + 8, :]
                    for e in range(3):
                        term = taps[27 * c + 9 * a + 3 * b + e] * v
                        acc[e] = term if acc[e] is None else acc[e] + term
        spread = beside(acc[2], acc[0], acc[1])
        at = slice(row, row + 8)
        first = weight_g * misfit[0, at, :] + spread
        return first, weight_m * misfit[1, at, :] * growth[0, at, :]

    for row in range(0, growth.shape[1], CHUNK):
        d0, m0 = part(row)
        d1, m1 = part(row + 8)
        at = slice(row, row + CHUNK)
        out_ref[0, 0, at, :] = jnp.concatenate([d0, d1], 0).astype(jnp.bfloat16)
        out_ref[1, 0, at, :] = jnp.concatenate([m0, m1], 0).astype(jnp.bfloat16)


def params():
    return pltpu.CompilerParams(
        dimension_semantics=("arbitrary",), vmem_limit_bytes=40 * 1024 * 1024
    )


def cost(cells, flops, size):
    return pl.CostEstimate(flops=cells * flops, bytes_accessed=cells * size, transcendentals=0)


def coupling_forward(rim, magnetic, taps, weights):
    depth, rows, cols = magnetic.shape
    tall = rim.shape[1]
    smem = pl.BlockSpec(memory_space=pltpu.SMEM)
    plane = [pl.BlockSpec((1, tall, cols), lambda z, a=a: (z + a, 0, 0)) for a in range(3)]
    cells = pl.BlockSpec((1, rows, cols), lambda z: (z, 0, 0))
    full = jax.ShapeDtypeStruct(magnetic.shape, jnp.float32)
    return pl.pallas_call(
        forward_kernel,
        grid=(depth,),
        in_specs=[smem, smem, *plane, cells],
        out_specs=[cells, cells, pl.BlockSpec((2, rows, cols), lambda z: (0, 0, 0))],
        out_shape=[full, full, jax.ShapeDtypeStruct((2, rows, cols), jnp.float32)],
        compiler_params=params(),
        cost_estimate=cost(depth * rows * cols, 120, 24),
    )(taps, weights, rim, rim, rim, magnetic)


def coupling_backward(outer, growth, misfit, taps, weights):
    depth, rows, cols = growth.shape
    tall = outer.shape[2]
    smem = pl.BlockSpec(memory_space=pltpu.SMEM)
    plane = [pl.BlockSpec((2, 1, tall, cols), lambda z, a=a: (0, z + a, 0, 0)) for a in range(3)]
    return pl.pallas_call(
        backward_kernel,
        grid=(depth,),
        in_specs=[
            smem,
            smem,
            *plane,
            pl.BlockSpec((1, rows, cols), lambda z: (z, 0, 0)),
            pl.BlockSpec((2, rows, cols), lambda z: (0, 0, 0)),
        ],
        out_specs=pl.BlockSpec((2, 1, rows, cols), lambda z: (0, z, 0, 0)),
        out_shape=jax.ShapeDtypeStruct((2, depth, rows, cols), jnp.bfloat16),
        compiler_params=params(),
        cost_estimate=cost(depth * rows * cols, 120, 32),
    )(taps, weights, outer, outer, outer, growth, misfit)


def depth_weights(first_row, depth_rows):
    depth = (first_row + jnp.arange(depth_rows)).astype(jnp.float32)
    factor = 4.0 / math.sqrt(NZ)
    return (factor / (1.0 + depth / NZ) ** 2, factor / (1.0 + depth / NZ) ** 3)


def local(whitened, observed, lower_x, lower_y, lower_z, coupling_kernel):
    factor_x, factor_y = (
        lax.all_gather(lower_x, "gx", axis=0, tiled=True),
        lax.all_gather(lower_y, "gx", axis=0, tiled=True),
    )

    def apply_depth(values):
        return jnp.einsum(
            "zk,fkxy->fzxy", lower_z, values, preferred_element_type=jnp.float32
        ).astype(jnp.bfloat16)

    def apply_across(values):
        return jnp.einsum(
            "xk,fzky->fzxy", factor_x, values, preferred_element_type=jnp.float32
        ).astype(jnp.bfloat16)

    def depth_adjoint(values):
        return jnp.einsum(
            "kz,fkxy->fzxy", lower_z, values, preferred_element_type=jnp.float32
        ).astype(jnp.bfloat16)

    def across_adjoint(values):
        return jnp.einsum(
            "kx,fzky->fzxy", factor_x, values, preferred_element_type=jnp.float32
        ).astype(jnp.bfloat16)

    def apply_lines(values):
        first = jnp.einsum(
            "fzxk,yk->fzxy", values, factor_y, preferred_element_type=jnp.float32
        ).astype(jnp.bfloat16)
        return apply_depth(first)

    start = whitened.astype(jnp.bfloat16)
    model = across_lines(depth_lines(start, apply_lines), apply_across)
    density, magnetic = model[0], model[1]
    depth_rows = density.shape[0]
    taps = coupling_kernel.reshape(-1)
    weight_g, weight_m = depth_weights(lax.axis_index("gz") * depth_rows, depth_rows)
    weights = jnp.stack([weight_g, weight_m])
    rim = edge_padded(padded_2(density, (("gx", 1), ("gz", 0)), 1))
    growth, slope, sums = coupling_forward(rim, magnetic, taps, weights)
    misfit = lax.psum(sums, "gz") - observed
    back_m = weight_m[:, None, None] * misfit[1][None]
    cotangents = jnp.stack([back_m * slope, back_m]).astype(jnp.bfloat16)
    outer = edge_padded(padded_2(cotangents, (("gx", 2), ("gz", 1)), 1))
    adjoint = coupling_backward(outer, growth, misfit, taps, weights)
    fourth = depth_lines(across_lines(adjoint, across_adjoint), depth_adjoint)
    gradient = whitened + jnp.einsum(
        "fzxk,ky->fzxy", fourth, factor_y, preferred_element_type=jnp.float32
    )
    return (gradient, misfit)


def solution(mesh):
    in_specs = (
        P(None, "gz", "gx", None),
        P(None, "gx", None),
        P("gx", None),
        P("gx", None),
        P(),
        P(),
    )
    out_specs = (P(None, "gz", "gx", None), P(None, "gx", None))
    return jax.shard_map(local, mesh=mesh, in_specs=in_specs, out_specs=out_specs, check_vma=False)
```

```python
import math

import jax
import jax.numpy as jnp
from jax import lax
from jax.experimental import pallas as pl
from jax.experimental.pallas import tpu as pltpu
from jax.sharding import PartitionSpec as P

NZ = 64


def padded_2(x, sides, width):
    for axis, dim in sides:
        peers, length = (lax.axis_size(axis), x.shape[dim])
        up = [(i, (i + 1) % peers) for i in range(peers - 1)]
        down = [(j, i) for i, j in up]
        last = lax.slice_in_dim(x, length - width, length, axis=dim)
        first = lax.slice_in_dim(x, 0, width, axis=dim)
        before = lax.ppermute(last, axis, up)
        after = lax.ppermute(first, axis, down)
        x = jnp.concatenate([before, x, after], axis=dim)
    return x


def moved(values, axis, split, concat):
    return lax.all_to_all(values, axis, split_axis=split, concat_axis=concat, tiled=True)


def total(values, axis):
    peers = lax.axis_size(axis)
    if peers & (peers - 1):
        return lax.psum(values, axis)
    step = 1
    while step < peers:
        values = values + lax.ppermute(values, axis, [(i, i ^ step) for i in range(peers)])
        step *= 2
    return values


def depth_lines(values, local_step):
    return moved(local_step(moved(values, "gz", 2, 1)), "gz", 1, 2)


def across_lines(values, local_step):
    if values.shape[1] % lax.axis_size("gx"):
        return moved(local_step(moved(values, "gx", 3, 2)), "gx", 2, 3)
    return moved(local_step(moved(values, "gx", 1, 2)), "gx", 2, 1)


CHUNK = 16
EDGE = 8


def edge_padded(rim):
    sides = ((EDGE - 1, EDGE - 1), (0, 0))
    return jnp.pad(rim, ((0, 0),) * (rim.ndim - 2) + sides).astype(jnp.float32)


def beside(low, high, middle):
    cols = middle.shape[1]
    lane = lax.broadcasted_iota(jnp.int32, middle.shape, 1)
    before = jnp.where(lane == 0, 0.0, pltpu.roll(low, 1, 1))
    after = jnp.where(lane == cols - 1, 0.0, pltpu.roll(high, cols - 1, 1))
    return middle + before + after


def forward_kernel(taps, weights, p0, p1, p2, growth_out, slope_out, sums):
    z = pl.program_id(0)
    planes = (p0, p1, p2)
    weight_g, weight_m = weights[0, z], weights[1, z]

    @pl.when(z == 0)
    def _():
        sums[...] = jnp.zeros_like(sums)

    for row in range(0, growth_out.shape[1], 8):
        acc = [None] * 6
        for a in range(3):
            for b in range(3):
                at = row + EDGE - 1 + b
                v = planes[a][0, at : at + 8, :]
                for c in range(2):
                    for e in range(3):
                        term = taps[27 * c + 9 * a + 3 * b + e] * v
                        i = 3 * c + e
                        acc[i] = term if acc[i] is None else acc[i] + term
        scale = jnp.tanh(beside(acc[0], acc[2], acc[1]))
        growth = jnp.exp(scale)
        out = slice(row, row + 8)
        growth_out[0, out, :] = growth
        slope_out[0, out, :] = growth * (1.0 - scale * scale)
        sums[0, out, :] += weight_g * p1[0, row + EDGE : row + EDGE + 8, :]
        sums[1, out, :] += weight_m * beside(acc[3], acc[5], acc[4])


def backward_kernel(taps, weights, p0, p1, p2, misfit, out_ref):
    z = pl.program_id(0)
    planes = (p2, p1, p0)

    def part(row):
        acc = [None] * 3
        for c in range(2):
            for a in range(3):
                for b in range(3):
                    at = row + EDGE + 1 - b
                    v = planes[a][c, 0, at : at + 8, :]
                    for e in range(3):
                        term = taps[27 * c + 9 * a + 3 * b + e] * v
                        acc[e] = term if acc[e] is None else acc[e] + term
        return weights[0, z] * misfit[row : row + 8, :] + beside(acc[2], acc[0], acc[1])

    for row in range(0, out_ref.shape[1], CHUNK):
        both = jnp.concatenate([part(row), part(row + 8)], 0)
        out_ref[0, row : row + CHUNK, :] = both.astype(jnp.bfloat16)


def params():
    return pltpu.CompilerParams(
        dimension_semantics=("arbitrary",), vmem_limit_bytes=40 * 1024 * 1024
    )


def cost(cells, flops, size):
    return pl.CostEstimate(flops=cells * flops, bytes_accessed=cells * size, transcendentals=0)


def coupling_forward(rim, taps, weights):
    depth, tall, cols = rim.shape[0] - 2, rim.shape[1], rim.shape[2]
    rows = tall - 2 * EDGE
    smem = pl.BlockSpec(memory_space=pltpu.SMEM)
    plane = [pl.BlockSpec((1, tall, cols), lambda z, a=a: (z + a, 0, 0)) for a in range(3)]
    cells = pl.BlockSpec((1, rows, cols), lambda z: (z, 0, 0))
    full = jax.ShapeDtypeStruct((depth, rows, cols), jnp.float32)
    return pl.pallas_call(
        forward_kernel,
        grid=(depth,),
        in_specs=[smem, smem, *plane],
        out_specs=[cells, cells, pl.BlockSpec((2, rows, cols), lambda z: (0, 0, 0))],
        out_shape=[full, full, jax.ShapeDtypeStruct((2, rows, cols), jnp.float32)],
        compiler_params=params(),
        cost_estimate=cost(depth * rows * cols, 1200, 24),
    )(taps, weights, rim, rim, rim)


def coupling_backward(outer, misfit, taps, weights):
    depth, tall, cols = outer.shape[1] - 2, outer.shape[2], outer.shape[3]
    rows = tall - 2 * EDGE
    smem = pl.BlockSpec(memory_space=pltpu.SMEM)
    plane = [pl.BlockSpec((2, 1, tall, cols), lambda z, a=a: (0, z + a, 0, 0)) for a in range(3)]
    return pl.pallas_call(
        backward_kernel,
        grid=(depth,),
        in_specs=[
            smem,
            smem,
            *plane,
            pl.BlockSpec((rows, cols), lambda z: (0, 0)),
        ],
        out_specs=pl.BlockSpec((1, rows, cols), lambda z: (z, 0, 0)),
        out_shape=jax.ShapeDtypeStruct((depth, rows, cols), jnp.bfloat16),
        compiler_params=params(),
        cost_estimate=cost(depth * rows * cols, 1200, 32),
    )(taps, weights, outer, outer, outer, misfit)


def depth_weights(first_row, depth_rows):
    depth = (first_row + jnp.arange(depth_rows)).astype(jnp.float32)
    factor = 4.0 / math.sqrt(NZ)
    return (factor / (1.0 + depth / NZ) ** 2, factor / (1.0 + depth / NZ) ** 3)


def local(whitened, observed, lower_x, lower_y, lower_z, coupling_kernel):
    factor_x, factor_y = (
        lax.all_gather(lower_x, "gx", axis=0, tiled=True),
        lax.all_gather(lower_y, "gx", axis=0, tiled=True),
    )

    def apply_depth(values):
        return jnp.einsum(
            "zk,fkxy->fzxy", lower_z, values, preferred_element_type=jnp.float32
        ).astype(jnp.bfloat16)

    def apply_across(values):
        return jnp.einsum(
            "xk,fzky->fzxy", factor_x, values, preferred_element_type=jnp.float32
        ).astype(jnp.bfloat16)

    def depth_adjoint(values):
        return jnp.einsum(
            "kz,fkxy->fzxy", lower_z, values, preferred_element_type=jnp.float32
        ).astype(jnp.bfloat16)

    def across_adjoint(values):
        return jnp.einsum(
            "kx,fzky->fzxy", factor_x, values, preferred_element_type=jnp.float32
        ).astype(jnp.bfloat16)

    def apply_lines(values):
        first = jnp.einsum(
            "fzxk,yk->fzxy", values, factor_y, preferred_element_type=jnp.float32
        ).astype(jnp.bfloat16)
        return apply_depth(first)

    start = whitened.astype(jnp.bfloat16)
    def to_model(field):
        return across_lines(depth_lines(start[field : field + 1], apply_lines), apply_across)[0]

    def to_gradient(field, adjoint):
        fourth = depth_lines(across_lines(adjoint[None], across_adjoint), depth_adjoint)
        return whitened[field : field + 1] + jnp.einsum(
            "fzxk,ky->fzxy", fourth, factor_y, preferred_element_type=jnp.float32
        )

    density = to_model(0)
    magnetic = to_model(1).astype(jnp.float32)
    depth_rows = density.shape[0]
    taps = coupling_kernel.reshape(-1)
    weight_g, weight_m = depth_weights(lax.axis_index("gz") * depth_rows, depth_rows)
    weights = jnp.stack([weight_g, weight_m])
    rim = edge_padded(padded_2(density, (("gx", 1), ("gz", 0)), 1))
    growth, slope, sums = coupling_forward(rim, taps, weights)
    part_m = sums[1] + jnp.sum(weight_m[:, None, None] * (magnetic * growth), axis=0)
    misfit_g = total(sums[0], "gz") - observed[0]
    misfit_m = total(part_m, "gz") - observed[1]
    back_m = weight_m[:, None, None] * misfit_m[None]
    gradient_m = to_gradient(1, (back_m * growth).astype(jnp.bfloat16))
    cotangents = jnp.stack([back_m * magnetic * slope, back_m]).astype(jnp.bfloat16)
    outer = edge_padded(padded_2(cotangents, (("gx", 2), ("gz", 1)), 1))
    gradient_g = to_gradient(0, coupling_backward(outer, misfit_g, taps, weights))
    return (jnp.concatenate([gradient_g, gradient_m]), jnp.stack([misfit_g, misfit_m]))


def solution(mesh):
    in_specs = (
        P(None, "gz", "gx", None),
        P(None, "gx", None),
        P("gx", None),
        P("gx", None),
        P(),
        P(),
    )
    out_specs = (P(None, "gz", "gx", None), P(None, "gx", None))
    return jax.shard_map(local, mesh=mesh, in_specs=in_specs, out_specs=out_specs, check_vma=False)
```

```python
import math

import jax
import jax.numpy as jnp
from jax import lax
from jax.experimental import pallas as pl
from jax.experimental.pallas import tpu as pltpu
from jax.sharding import PartitionSpec as P

NZ = 64


def padded_2(x, sides, width):
    for axis, dim in sides:
        peers, length = (lax.axis_size(axis), x.shape[dim])
        up = [(i, (i + 1) % peers) for i in range(peers - 1)]
        down = [(j, i) for i, j in up]
        last = lax.slice_in_dim(x, length - width, length, axis=dim)
        first = lax.slice_in_dim(x, 0, width, axis=dim)
        before = lax.ppermute(last, axis, up)
        after = lax.ppermute(first, axis, down)
        x = jnp.concatenate([before, x, after], axis=dim)
    return x


def moved(values, axis, split, concat):
    peers, me = lax.axis_size(axis), lax.axis_index(axis)
    if axis == "gx" or peers > 8:
        return lax.all_to_all(values, axis, split_axis=split, concat_axis=concat, tiled=True)
    width, length = values.shape[split] // peers, values.shape[concat]

    def piece(owner):
        return lax.dynamic_slice_in_dim(values, owner * width, width, axis=split)

    shape = list(values.shape)
    shape[split], shape[concat] = width, length * peers
    parts = [(me, piece(me))]
    for step in range(1, peers):
        ring = [(i, (i + step) % peers) for i in range(peers)]
        sent = lax.ppermute(piece(lax.rem(me + step, peers)), axis, ring)
        parts.append((lax.rem(me + peers - step, peers), sent))
    whole = jnp.zeros(shape, values.dtype)
    for owner, part in parts:
        whole = lax.dynamic_update_slice_in_dim(whole, part, owner * length, axis=concat)
    return whole


def total(values, axis):
    peers = lax.axis_size(axis)
    if peers & (peers - 1):
        return lax.psum(values, axis)
    step = 1
    while step < peers:
        values = values + lax.ppermute(values, axis, [(i, i ^ step) for i in range(peers)])
        step *= 2
    return values


def depth_lines(values, local_step):
    return moved(local_step(moved(values, "gz", 2, 1)), "gz", 1, 2)


def across_lines(values, local_step):
    if values.shape[1] % lax.axis_size("gx"):
        return moved(local_step(moved(values, "gx", 3, 2)), "gx", 2, 3)
    return moved(local_step(moved(values, "gx", 1, 2)), "gx", 2, 1)


CHUNK = 16
EDGE = 8


def edge_padded(rim):
    sides = ((EDGE - 1, EDGE - 1), (0, 0))
    return jnp.pad(rim, ((0, 0),) * (rim.ndim - 2) + sides).astype(jnp.float32)


def beside(low, high, middle):
    cols = middle.shape[1]
    lane = lax.broadcasted_iota(jnp.int32, middle.shape, 1)
    before = jnp.where(lane == 0, 0.0, pltpu.roll(low, 1, 1))
    after = jnp.where(lane == cols - 1, 0.0, pltpu.roll(high, cols - 1, 1))
    return middle + before + after


def forward_kernel(taps, weights, p0, p1, p2, growth_out, slope_out, sums):
    z = pl.program_id(0)
    planes = (p0, p1, p2)
    weight_g, weight_m = weights[0, z], weights[1, z]

    @pl.when(z == 0)
    def _():
        sums[...] = jnp.zeros_like(sums)

    for row in range(0, growth_out.shape[1], 8):
        acc = [None] * 6
        for a in range(3):
            for b in range(3):
                at = row + EDGE - 1 + b
                v = planes[a][0, at : at + 8, :]
                for c in range(2):
                    for e in range(3):
                        term = taps[27 * c + 9 * a + 3 * b + e] * v
                        i = 3 * c + e
                        acc[i] = term if acc[i] is None else acc[i] + term
        scale = jnp.tanh(beside(acc[0], acc[2], acc[1]))
        growth = jnp.exp(scale)
        out = slice(row, row + 8)
        growth_out[0, out, :] = growth
        slope_out[0, out, :] = growth * (1.0 - scale * scale)
        sums[0, out, :] += weight_g * p1[0, row + EDGE : row + EDGE + 8, :]
        sums[1, out, :] += weight_m * beside(acc[3], acc[5], acc[4])


def backward_kernel(taps, weights, p0, p1, p2, misfit, out_ref):
    z = pl.program_id(0)
    planes = (p2, p1, p0)

    def part(row):
        acc = [None] * 3
        for c in range(2):
            for a in range(3):
                for b in range(3):
                    at = row + EDGE + 1 - b
                    v = planes[a][c, 0, at : at + 8, :]
                    for e in range(3):
                        term = taps[27 * c + 9 * a + 3 * b + e] * v
                        acc[e] = term if acc[e] is None else acc[e] + term
        return weights[0, z] * misfit[row : row + 8, :] + beside(acc[2], acc[0], acc[1])

    for row in range(0, out_ref.shape[1], CHUNK):
        both = jnp.concatenate([part(row), part(row + 8)], 0)
        out_ref[0, row : row + CHUNK, :] = both.astype(jnp.bfloat16)


def params():
    return pltpu.CompilerParams(
        dimension_semantics=("arbitrary",), vmem_limit_bytes=40 * 1024 * 1024
    )


def cost(cells, flops, size):
    return pl.CostEstimate(flops=cells * flops, bytes_accessed=cells * size, transcendentals=0)


def coupling_forward(rim, taps, weights):
    depth, tall, cols = rim.shape[0] - 2, rim.shape[1], rim.shape[2]
    rows = tall - 2 * EDGE
    smem = pl.BlockSpec(memory_space=pltpu.SMEM)
    plane = [pl.BlockSpec((1, tall, cols), lambda z, a=a: (z + a, 0, 0)) for a in range(3)]
    cells = pl.BlockSpec((1, rows, cols), lambda z: (z, 0, 0))
    full = jax.ShapeDtypeStruct((depth, rows, cols), jnp.float32)
    return pl.pallas_call(
        forward_kernel,
        grid=(depth,),
        in_specs=[smem, smem, *plane],
        out_specs=[cells, cells, pl.BlockSpec((2, rows, cols), lambda z: (0, 0, 0))],
        out_shape=[full, full, jax.ShapeDtypeStruct((2, rows, cols), jnp.float32)],
        compiler_params=params(),
        cost_estimate=cost(depth * rows * cols, 1200, 24),
    )(taps, weights, rim, rim, rim)


def coupling_backward(outer, misfit, taps, weights):
    depth, tall, cols = outer.shape[1] - 2, outer.shape[2], outer.shape[3]
    rows = tall - 2 * EDGE
    smem = pl.BlockSpec(memory_space=pltpu.SMEM)
    plane = [pl.BlockSpec((2, 1, tall, cols), lambda z, a=a: (0, z + a, 0, 0)) for a in range(3)]
    return pl.pallas_call(
        backward_kernel,
        grid=(depth,),
        in_specs=[
            smem,
            smem,
            *plane,
            pl.BlockSpec((rows, cols), lambda z: (0, 0)),
        ],
        out_specs=pl.BlockSpec((1, rows, cols), lambda z: (z, 0, 0)),
        out_shape=jax.ShapeDtypeStruct((depth, rows, cols), jnp.bfloat16),
        compiler_params=params(),
        cost_estimate=cost(depth * rows * cols, 1200, 32),
    )(taps, weights, outer, outer, outer, misfit)


def depth_weights(first_row, depth_rows):
    depth = (first_row + jnp.arange(depth_rows)).astype(jnp.float32)
    factor = 4.0 / math.sqrt(NZ)
    return (factor / (1.0 + depth / NZ) ** 2, factor / (1.0 + depth / NZ) ** 3)


def local(whitened, observed, lower_x, lower_y, lower_z, coupling_kernel):
    factor_x, factor_y = (
        lax.all_gather(lower_x, "gx", axis=0, tiled=True),
        lax.all_gather(lower_y, "gx", axis=0, tiled=True),
    )

    def apply_depth(values):
        return jnp.einsum(
            "zk,fkxy->fzxy", lower_z, values, preferred_element_type=jnp.float32
        ).astype(jnp.bfloat16)

    def apply_across(values):
        return jnp.einsum(
            "xk,fzky->fzxy", factor_x, values, preferred_element_type=jnp.float32
        ).astype(jnp.bfloat16)

    def depth_adjoint(values):
        return jnp.einsum(
            "kz,fkxy->fzxy", lower_z, values, preferred_element_type=jnp.float32
        ).astype(jnp.bfloat16)

    def across_adjoint(values):
        return jnp.einsum(
            "kx,fzky->fzxy", factor_x, values, preferred_element_type=jnp.float32
        ).astype(jnp.bfloat16)

    def apply_lines(values):
        first = jnp.einsum(
            "fzxk,yk->fzxy", values, factor_y, preferred_element_type=jnp.float32
        ).astype(jnp.bfloat16)
        return apply_depth(first)

    start = whitened.astype(jnp.bfloat16)
    def to_model(field):
        return across_lines(depth_lines(start[field : field + 1], apply_lines), apply_across)[0]

    def to_gradient(field, adjoint):
        fourth = depth_lines(across_lines(adjoint[None], across_adjoint), depth_adjoint)
        return whitened[field : field + 1] + jnp.einsum(
            "fzxk,ky->fzxy", fourth, factor_y, preferred_element_type=jnp.float32
        )

    density = to_model(0)
    magnetic = to_model(1).astype(jnp.float32)
    depth_rows = density.shape[0]
    taps = coupling_kernel.reshape(-1)
    weight_g, weight_m = depth_weights(lax.axis_index("gz") * depth_rows, depth_rows)
    weights = jnp.stack([weight_g, weight_m])
    rim = edge_padded(padded_2(density, (("gx", 1), ("gz", 0)), 1))
    growth, slope, sums = coupling_forward(rim, taps, weights)
    part_m = sums[1] + jnp.sum(weight_m[:, None, None] * (magnetic * growth), axis=0)
    misfit_g = total(sums[0], "gz") - observed[0]
    misfit_m = total(part_m, "gz") - observed[1]
    back_m = weight_m[:, None, None] * misfit_m[None]
    gradient_m = to_gradient(1, (back_m * growth).astype(jnp.bfloat16))
    cotangents = jnp.stack([back_m * magnetic * slope, back_m]).astype(jnp.bfloat16)
    outer = edge_padded(padded_2(cotangents, (("gx", 2), ("gz", 1)), 1))
    gradient_g = to_gradient(0, coupling_backward(outer, misfit_g, taps, weights))
    return (jnp.concatenate([gradient_g, gradient_m]), jnp.stack([misfit_g, misfit_m]))


def solution(mesh):
    in_specs = (
        P(None, "gz", "gx", None),
        P(None, "gx", None),
        P("gx", None),
        P("gx", None),
        P(),
        P(),
    )
    out_specs = (P(None, "gz", "gx", None), P(None, "gx", None))
    return jax.shard_map(local, mesh=mesh, in_specs=in_specs, out_specs=out_specs, check_vma=False)
```

```python
import math

import jax
import jax.numpy as jnp
from jax import lax
from jax.experimental import pallas as pl
from jax.experimental.pallas import tpu as pltpu
from jax.sharding import PartitionSpec as P

NZ = 64


def padded_2(x, sides, width):
    for axis, dim in sides:
        peers, length = (lax.axis_size(axis), x.shape[dim])
        up = [(i, (i + 1) % peers) for i in range(peers - 1)]
        down = [(j, i) for i, j in up]
        last = lax.slice_in_dim(x, length - width, length, axis=dim)
        first = lax.slice_in_dim(x, 0, width, axis=dim)
        before = lax.ppermute(last, axis, up)
        after = lax.ppermute(first, axis, down)
        x = jnp.concatenate([before, x, after], axis=dim)
    return x


def moved(values, axis, split, concat):
    peers, me = lax.axis_size(axis), lax.axis_index(axis)
    if axis == "gx" or peers > 8:
        return lax.all_to_all(values, axis, split_axis=split, concat_axis=concat, tiled=True)
    width, length = values.shape[split] // peers, values.shape[concat]

    def piece(owner):
        return lax.dynamic_slice_in_dim(values, owner * width, width, axis=split)

    shape = list(values.shape)
    shape[split], shape[concat] = width, length * peers
    parts = [(me, piece(me))]
    for step in range(1, peers):
        ring = [(i, (i + step) % peers) for i in range(peers)]
        sent = lax.ppermute(piece(lax.rem(me + step, peers)), axis, ring)
        parts.append((lax.rem(me + peers - step, peers), sent))
    whole = jnp.zeros(shape, values.dtype)
    for owner, part in parts:
        whole = lax.dynamic_update_slice_in_dim(whole, part, owner * length, axis=concat)
    return whole


def gathered(values, axis):
    peers, me = lax.axis_size(axis), lax.axis_index(axis)
    if peers > 8:
        return lax.all_gather(values, axis, axis=0, tiled=True)
    rows = values.shape[0]
    whole = jnp.zeros((rows * peers,) + values.shape[1:], values.dtype)
    whole = lax.dynamic_update_slice_in_dim(whole, values, me * rows, axis=0)
    for step in range(1, peers):
        ring = [(i, (i + step) % peers) for i in range(peers)]
        owner = lax.rem(me + peers - step, peers)
        part = lax.ppermute(values, axis, ring)
        whole = lax.dynamic_update_slice_in_dim(whole, part, owner * rows, axis=0)
    return whole


def total(values, axis):
    peers = lax.axis_size(axis)
    if peers & (peers - 1):
        return lax.psum(values, axis)
    step = 1
    while step < peers:
        values = values + lax.ppermute(values, axis, [(i, i ^ step) for i in range(peers)])
        step *= 2
    return values


def depth_lines(values, local_step):
    return moved(local_step(moved(values, "gz", 2, 1)), "gz", 1, 2)


def across_lines(values, local_step):
    if values.shape[1] % lax.axis_size("gx"):
        return moved(local_step(moved(values, "gx", 3, 2)), "gx", 2, 3)
    return moved(local_step(moved(values, "gx", 1, 2)), "gx", 2, 1)


CHUNK = 16
EDGE = 8


def edge_padded(rim):
    sides = ((EDGE - 1, EDGE - 1), (0, 0))
    return jnp.pad(rim, ((0, 0),) * (rim.ndim - 2) + sides).astype(jnp.float32)


def beside(low, high, middle):
    cols = middle.shape[1]
    lane = lax.broadcasted_iota(jnp.int32, middle.shape, 1)
    before = jnp.where(lane == 0, 0.0, pltpu.roll(low, 1, 1))
    after = jnp.where(lane == cols - 1, 0.0, pltpu.roll(high, cols - 1, 1))
    return middle + before + after


def forward_kernel(taps, weights, p0, p1, p2, growth_out, slope_out, sums):
    z = pl.program_id(0)
    planes = (p0, p1, p2)
    weight_g, weight_m = weights[0, z], weights[1, z]

    @pl.when(z == 0)
    def _():
        sums[...] = jnp.zeros_like(sums)

    for row in range(0, growth_out.shape[1], 8):
        acc = [None] * 6
        for a in range(3):
            for b in range(3):
                at = row + EDGE - 1 + b
                v = planes[a][0, at : at + 8, :]
                for c in range(2):
                    for e in range(3):
                        term = taps[27 * c + 9 * a + 3 * b + e] * v
                        i = 3 * c + e
                        acc[i] = term if acc[i] is None else acc[i] + term
        scale = jnp.tanh(beside(acc[0], acc[2], acc[1]))
        growth = jnp.exp(scale)
        out = slice(row, row + 8)
        growth_out[0, out, :] = growth
        slope_out[0, out, :] = growth * (1.0 - scale * scale)
        sums[0, out, :] += weight_g * p1[0, row + EDGE : row + EDGE + 8, :]
        sums[1, out, :] += weight_m * beside(acc[3], acc[5], acc[4])


def backward_kernel(taps, weights, p0, p1, p2, misfit, out_ref):
    z = pl.program_id(0)
    planes = (p2, p1, p0)

    def part(row):
        acc = [None] * 3
        for c in range(2):
            for a in range(3):
                for b in range(3):
                    at = row + EDGE + 1 - b
                    v = planes[a][c, 0, at : at + 8, :]
                    for e in range(3):
                        term = taps[27 * c + 9 * a + 3 * b + e] * v
                        acc[e] = term if acc[e] is None else acc[e] + term
        return weights[0, z] * misfit[row : row + 8, :] + beside(acc[2], acc[0], acc[1])

    for row in range(0, out_ref.shape[1], CHUNK):
        both = jnp.concatenate([part(row), part(row + 8)], 0)
        out_ref[0, row : row + CHUNK, :] = both.astype(jnp.bfloat16)


def params():
    return pltpu.CompilerParams(
        dimension_semantics=("arbitrary",), vmem_limit_bytes=40 * 1024 * 1024
    )


def cost(cells, flops, size):
    return pl.CostEstimate(flops=cells * flops, bytes_accessed=cells * size, transcendentals=0)


def coupling_forward(rim, taps, weights):
    depth, tall, cols = rim.shape[0] - 2, rim.shape[1], rim.shape[2]
    rows = tall - 2 * EDGE
    smem = pl.BlockSpec(memory_space=pltpu.SMEM)
    plane = [pl.BlockSpec((1, tall, cols), lambda z, a=a: (z + a, 0, 0)) for a in range(3)]
    cells = pl.BlockSpec((1, rows, cols), lambda z: (z, 0, 0))
    full = jax.ShapeDtypeStruct((depth, rows, cols), jnp.float32)
    return pl.pallas_call(
        forward_kernel,
        grid=(depth,),
        in_specs=[smem, smem, *plane],
        out_specs=[cells, cells, pl.BlockSpec((2, rows, cols), lambda z: (0, 0, 0))],
        out_shape=[full, full, jax.ShapeDtypeStruct((2, rows, cols), jnp.float32)],
        compiler_params=params(),
        cost_estimate=cost(depth * rows * cols, 1200, 24),
    )(taps, weights, rim, rim, rim)


def coupling_backward(outer, misfit, taps, weights):
    depth, tall, cols = outer.shape[1] - 2, outer.shape[2], outer.shape[3]
    rows = tall - 2 * EDGE
    smem = pl.BlockSpec(memory_space=pltpu.SMEM)
    plane = [pl.BlockSpec((2, 1, tall, cols), lambda z, a=a: (0, z + a, 0, 0)) for a in range(3)]
    return pl.pallas_call(
        backward_kernel,
        grid=(depth,),
        in_specs=[
            smem,
            smem,
            *plane,
            pl.BlockSpec((rows, cols), lambda z: (0, 0)),
        ],
        out_specs=pl.BlockSpec((1, rows, cols), lambda z: (z, 0, 0)),
        out_shape=jax.ShapeDtypeStruct((depth, rows, cols), jnp.bfloat16),
        compiler_params=params(),
        cost_estimate=cost(depth * rows * cols, 1200, 32),
    )(taps, weights, outer, outer, outer, misfit)


def depth_weights(first_row, depth_rows):
    depth = (first_row + jnp.arange(depth_rows)).astype(jnp.float32)
    factor = 4.0 / math.sqrt(NZ)
    return (factor / (1.0 + depth / NZ) ** 2, factor / (1.0 + depth / NZ) ** 3)


def local(whitened, observed, lower_x, lower_y, lower_z, coupling_kernel):
    factor_x, factor_y = (
        gathered(lower_x, "gx"),
        lax.all_gather(lower_y, "gx", axis=0, tiled=True),
    )

    def apply_depth(values):
        return jnp.einsum(
            "zk,fkxy->fzxy", lower_z, values, preferred_element_type=jnp.float32
        ).astype(jnp.bfloat16)

    def apply_across(values):
        return jnp.einsum(
            "xk,fzky->fzxy", factor_x, values, preferred_element_type=jnp.float32
        ).astype(jnp.bfloat16)

    def depth_adjoint(values):
        return jnp.einsum(
            "kz,fkxy->fzxy", lower_z, values, preferred_element_type=jnp.float32
        ).astype(jnp.bfloat16)

    def across_adjoint(values):
        return jnp.einsum(
            "kx,fzky->fzxy", factor_x, values, preferred_element_type=jnp.float32
        ).astype(jnp.bfloat16)

    def apply_lines(values):
        first = jnp.einsum(
            "fzxk,yk->fzxy", values, factor_y, preferred_element_type=jnp.float32
        ).astype(jnp.bfloat16)
        return apply_depth(first)

    start = whitened.astype(jnp.bfloat16)
    def to_model(field):
        return across_lines(depth_lines(start[field : field + 1], apply_lines), apply_across)[0]

    def to_gradient(field, adjoint):
        fourth = depth_lines(across_lines(adjoint[None], across_adjoint), depth_adjoint)
        return whitened[field : field + 1] + jnp.einsum(
            "fzxk,ky->fzxy", fourth, factor_y, preferred_element_type=jnp.float32
        )

    density = to_model(0)
    magnetic = to_model(1).astype(jnp.float32)
    depth_rows = density.shape[0]
    taps = coupling_kernel.reshape(-1)
    weight_g, weight_m = depth_weights(lax.axis_index("gz") * depth_rows, depth_rows)
    weights = jnp.stack([weight_g, weight_m])
    rim = edge_padded(padded_2(density, (("gx", 1), ("gz", 0)), 1))
    growth, slope, sums = coupling_forward(rim, taps, weights)
    part_m = sums[1] + jnp.sum(weight_m[:, None, None] * (magnetic * growth), axis=0)
    misfit_g = total(sums[0], "gz") - observed[0]
    misfit_m = total(part_m, "gz") - observed[1]
    back_m = weight_m[:, None, None] * misfit_m[None]
    gradient_m = to_gradient(1, (back_m * growth).astype(jnp.bfloat16))
    cotangents = jnp.stack([back_m * magnetic * slope, back_m]).astype(jnp.bfloat16)
    outer = edge_padded(padded_2(cotangents, (("gx", 2), ("gz", 1)), 1))
    gradient_g = to_gradient(0, coupling_backward(outer, misfit_g, taps, weights))
    return (jnp.concatenate([gradient_g, gradient_m]), jnp.stack([misfit_g, misfit_m]))


def solution(mesh):
    in_specs = (
        P(None, "gz", "gx", None),
        P(None, "gx", None),
        P("gx", None),
        P("gx", None),
        P(),
        P(),
    )
    out_specs = (P(None, "gz", "gx", None), P(None, "gx", None))
    return jax.shard_map(local, mesh=mesh, in_specs=in_specs, out_specs=out_specs, check_vma=False)
```
